256 devices in a mesh: dp: 32 (over z_hi, x, core), sp: 8 (over y, z_lo).
Axes of the slice: x: 4, y: 4, z: 8 (z_hi: 4, z_lo: 2; z = z_hi * 2 + z_lo), core: 2. Of those that a mesh axis runs over, the one named last changes fastest.
Arguments:
- qkv_video: bfloat16 [64, 3, 768, 2048], P('dp', None, 'sp'), may hold values from -6 to 6
- qkv_text: bfloat16 [64, 3, 128, 2048], P('dp', None, None, 'sp'), may hold values from -6 to 6
- qk_gains: float32 [2, 2, 128], replicated, may hold values from 0.5 to 9
- text_len: int32 [64], P('dp'), may hold values from 32 to 128, as said below
- w_out_video: bfloat16 [2048, 3072], P('sp', 'dp'), may hold values from -0.125 to 0.125
- w_out_text: bfloat16 [2048, 3072], P('sp', 'dp'), may hold values from -0.125 to 0.125
- cot_video: bfloat16 [64, 768, 3072], P('dp', 'sp'), may hold values from -6 to 6
- cot_text: bfloat16 [64, 128, 3072], P('dp', None, 'sp'), may hold values from -6 to 6
Outputs:
- grad_qkv_video: bfloat16 [64, 3, 768, 2048], P('dp', None, 'sp')
- grad_qkv_text: bfloat16 [64, 3, 128, 2048], P('dp', None, None, 'sp')
- grad_w_video: float32 [2048, 3072], P('sp', 'dp')
- grad_w_text: float32 [2048, 3072], P('sp', 'dp')
The draws below stay inside these ranges and needn't reach their ends.
Inputs may be any that keep to these rules, and one draw needn't show every extreme that they name: `text_len`: the first clip holds 128 unpadded text tokens.
All inputs are finite; a program needn't handle non-finite values.
Results may differ from the reference program's by a relative error of at most 0.006.
The reference program's roundings to bfloat16 on the way count: a program that leaves them out, or rounds other values in their place, can miss the bound.
Values may be sent and summed in bfloat16 or wider, within the bound.
No kernel may reach another device: no remote copies, remote signals or barrier semaphores. Data moves between devices by JAX's collectives and lax.ppermute only.
A program may use at most 128 MiB of HBM per device.

```python
import jax
import jax.numpy as jnp
from jax import lax

D = 3072
H = 16
DH = 128
TXT = 128
VID = 768
CLIPS = 64


def draw_qk_gains(key, part):
    key = jax.random.fold_in(key, 11)
    return jax.random.uniform(key, (2, 2, DH), jnp.float32, 0.5, 2.0)


def draw_text_len(key, part):
    key = jax.random.fold_in(key, 12)
    drawn = jax.random.randint(key, (CLIPS,), TXT // 4, TXT + 1, dtype=jnp.int32)
    return drawn.at[0].set(TXT)


def raised(values, stream_key, source, target, parts, factor):
    def block_of(position):
        return (jnp.arange(values.shape[position]) // (values.shape[position] // parts)).reshape((-1,) + (1,) * (values.ndim - 1 - position))

    near = jax.random.permutation(stream_key, parts)[block_of(target)]
    far = (block_of(target) + parts // 2) % parts
    return jnp.where((block_of(source) == near) | (block_of(source) == far), factor * values, values)


def steps_of(rng, shape, split, low, largest):
    level, own = 1.0, jax.random.fold_in(rng, 6)
    for dim, parts in split:
        steps = jnp.exp(jax.random.uniform(jax.random.fold_in(own, dim), (parts,), jnp.float32, low / len(split), largest / len(split)))
        level = level * jnp.repeat(steps, shape[dim] // parts).reshape([-1 if axis == dim else 1 for axis in range(len(shape))])
    return level


def noise(rng, shape, scale, reach, cuts=(), kind=jnp.bfloat16):
    array = scale * jax.random.normal(rng, shape, jnp.float32)
    if cuts:
        array = array * steps_of(rng, shape, cuts, -0.22, 0.18)
    return jnp.clip(array, -reach, reach).astype(kind)


def bell_draw_with(key, dims, scale, limit, split, heavy, kind=jnp.bfloat16):
    entries = scale * jax.random.normal(key, dims, jnp.float32)
    if split:
        entries = entries * steps_of(key, dims, split, -0.22, 0.18)
    return jnp.clip(raised(entries, jax.random.fold_in(key, 3), *heavy), -limit, limit).astype(kind)


def setup_inputs(seed: int = 0) -> dict:
    arg_keys = jax.random.split(jax.random.key(seed), 9)
    return {
        "qkv_video": noise(arg_keys[0], (CLIPS, 3, VID, H * DH), 1.0, 6.0, ((0, 32), (2, 8))),
        "qkv_text": noise(arg_keys[1], (CLIPS, 3, TXT, H * DH), 1.0, 6.0, ((0, 32), (3, 8))),
        "qk_gains": draw_qk_gains(jax.random.fold_in(arg_keys[8], 71), 0),
        "text_len": draw_text_len(jax.random.fold_in(arg_keys[8], 71), 0),
        "w_out_video": noise(arg_keys[4], (H * DH, D), (H * DH) ** -0.5, 0.125, ((0, 8), (1, 32))),
        "w_out_text": noise(arg_keys[5], (H * DH, D), (H * DH) ** -0.5, 0.125, ((0, 8), (1, 32))),
        "cot_video": bell_draw_with(arg_keys[6], (CLIPS, VID, D), 1.0, 6.0, ((0, 32), (1, 8)), (0, 2, 32, 2.75)),
        "cot_text": bell_draw_with(arg_keys[7], (CLIPS, TXT, D), 1.0, 6.0, ((0, 32), (2, 8)), (0, 2, 32, 2.75)),
    }


def norm_forward(raw_rows, gain_vec):
    per_head = raw_rows.astype(jnp.float32).reshape(raw_rows.shape[0], -1, DH)
    inverse = lax.rsqrt(lax.optimization_barrier(jnp.mean(per_head * per_head, axis=-1, keepdims=True)) + 1e-06)
    unit_vec = per_head * inverse
    return (unit_vec, inverse, (unit_vec * gain_vec).astype(jnp.bfloat16))

def norm_backward(unit_vec, inverse, gain_vec, incoming):
    scaled = incoming * gain_vec
    return inverse * (scaled - unit_vec * lax.optimization_barrier(jnp.mean(scaled * unit_vec, axis=-1, keepdims=True)))

def attention_setup(video, text, length, gains):
    video_len = video.shape[1]
    query_video = norm_forward(video[0], gains[0, 0])
    key_video = norm_forward(video[1], gains[0, 1])
    query_text = norm_forward(text[0], gains[1, 0])
    key_text = norm_forward(text[1], gains[1, 1])
    queries = jnp.concatenate([query_video[2], query_text[2]], axis=0)
    all_keys = jnp.concatenate([key_video[2], key_text[2]], axis=0)
    all_values = jnp.concatenate([video[2], text[2]], axis=0)
    all_values = all_values.reshape(all_values.shape[0], -1, DH)
    seq_len = queries.shape[0]
    visible = jnp.arange(seq_len, dtype=jnp.int32) < video_len + length
    scores = jnp.einsum('qhd,khd->hqk', queries.astype(jnp.float32), all_keys.astype(jnp.float32)) * DH ** (-0.5)
    scores = jnp.where(visible[None, None, :], scores, -1e+30)
    highest = lax.optimization_barrier(jnp.max(scores, axis=-1, keepdims=True))
    powers = jnp.exp(scores - highest)
    probability = powers / lax.optimization_barrier(jnp.sum(powers, axis=-1, keepdims=True))
    norms = (query_video, key_video, query_text, key_text)
    return (probability, queries, all_keys, all_values, norms)

def attend_forward(video, text, length, gains):
    probability, queries, all_keys, all_values, norms = attention_setup(video, text, length, gains)
    prob_low = probability.astype(jnp.bfloat16)
    attended = jnp.einsum('hqk,khd->qhd', prob_low.astype(jnp.float32), all_values.astype(jnp.float32))
    return attended.reshape(attended.shape[0], -1).astype(jnp.bfloat16)

def attend_backward(video, text, length, gains, grad_out):
    probability, queries, all_keys, all_values, norms = attention_setup(video, text, length, gains)
    prob_low = probability.astype(jnp.bfloat16)
    grad_rows = grad_out.reshape(grad_out.shape[0], -1, DH)
    grad_prob = jnp.einsum('qhd,khd->hqk', grad_rows.astype(jnp.float32), all_values.astype(jnp.float32))
    grad_score = probability * (grad_prob - lax.optimization_barrier(jnp.sum(probability * grad_prob, axis=-1, keepdims=True))) * DH ** (-0.5)
    score_low = grad_score.astype(jnp.bfloat16).astype(jnp.float32)
    grad_query = jnp.einsum('hqk,khd->qhd', score_low, all_keys.astype(jnp.float32))
    grad_key = jnp.einsum('hqk,qhd->khd', score_low, queries.astype(jnp.float32))
    grad_value = jnp.einsum('hqk,qhd->khd', prob_low.astype(jnp.float32), grad_rows.astype(jnp.float32))
    video_len = video.shape[1]
    query_video, key_video, query_text, key_text = norms
    video_grad = jnp.stack([norm_backward(query_video[0], query_video[1], gains[0, 0], grad_query[:video_len]), norm_backward(key_video[0], key_video[1], gains[0, 1], grad_key[:video_len]), grad_value[:video_len]])
    text_grad = jnp.stack([norm_backward(query_text[0], query_text[1], gains[1, 0], grad_query[video_len:]), norm_backward(key_text[0], key_text[1], gains[1, 1], grad_key[video_len:]), grad_value[video_len:]])
    video_grad = video_grad.reshape(3, video_len, -1).astype(jnp.bfloat16)
    text_grad = text_grad.reshape(3, text.shape[1], -1).astype(jnp.bfloat16)
    return (video_grad, text_grad)

def reference(qkv_video, qkv_text, qk_gains, text_len, w_out_video, w_out_text, cot_video, cot_text):
    grad_out_video = jnp.einsum('cvd,hd->cvh', cot_video.astype(jnp.float32), w_out_video.astype(jnp.float32)).astype(jnp.bfloat16)
    grad_out_text = jnp.einsum('ctd,hd->cth', cot_text.astype(jnp.float32), w_out_text.astype(jnp.float32)).astype(jnp.bfloat16)
    grad_out = jnp.concatenate([grad_out_video, grad_out_text], axis=1)

    def one_clip(packed):
        video, text, length, clip_grad = packed
        attended = attend_forward(video, text, length, qk_gains)
        video_grad, text_grad = attend_backward(video, text, length, qk_gains, clip_grad)
        return (attended, video_grad, text_grad)
    attended, grad_qkv_video, grad_qkv_text = lax.map(one_clip, (qkv_video, qkv_text, text_len, grad_out))
    video_len = qkv_video.shape[2]
    grad_w_video = jnp.einsum('cvh,cvd->hd', attended[:, :video_len].astype(jnp.float32), cot_video.astype(jnp.float32))
    grad_w_text = jnp.einsum('cth,ctd->hd', attended[:, video_len:].astype(jnp.float32), cot_text.astype(jnp.float32))
    return (grad_qkv_video, grad_qkv_text, grad_w_video, grad_w_text)
```

```python
import functools

import jax
import jax.numpy as jnp
from jax import lax
from jax.experimental import pallas as pl
from jax.experimental.pallas import tpu as pltpu
from jax.sharding import PartitionSpec as P

DH = 128
VID = 768
TXT = 128
SEQ = VID + TXT
BLK = 96
BF = jnp.bfloat16
F32 = jnp.float32
SCALE = DH ** (-0.5)
RELS = [(dy, dz) for dy in range(4) for dz in range(2)]
ANY = pl.BlockSpec(memory_space=pl.ANY)
SMEM = pl.BlockSpec(memory_space=pltpu.SMEM)
MB = 1024 * 1024


def shape_of(*dims, dtype=BF):
    return jax.ShapeDtypeStruct(dims, dtype)


def params(mb):
    return pltpu.CompilerParams(vmem_limit_bytes=mb * MB)


def cost(flops, nbytes, exps=0):
    return pl.CostEstimate(flops=flops, bytes_accessed=nbytes, transcendentals=exps)


def sp_perm(dy, dz):
    return [(y * 2 + z, ((y + dy) % 4) * 2 + (z + dz) % 2) for y in range(4) for z in range(2)]


def send_sp(value, dy, dz):
    return lax.ppermute(value, "sp", sp_perm(dy, dz))


def dp_perm(dh, dx, dc):
    return [
        ((h * 4 + x) * 2 + c, (((h + dh) % 4) * 4 + (x + dx) % 4) * 2 + (c + dc) % 2)
        for h in range(4)
        for x in range(4)
        for c in range(2)
    ]


def send_dp(value, dh, dx, dc):
    return lax.ppermute(value, "dp", dp_perm(dh, dx, dc))


def head_cols(yy, zz, half):
    return pl.multiple_of(yy * 512 + lax.rem(zz + half, 2) * 256, 256)


def relative_places(idx):
    y, zl = idx[0], idx[1]
    for k, (dy, dz) in enumerate(RELS):
        yy, zz = lax.rem(y + dy, 4), lax.rem(zl + dz, 2)
        for half in range(2):
            yield k, zz, half, pl.ds(head_cols(yy, zz, half), 256)


def pack_kernel(idx, qkv, cot, qt, ct, *rest):
    outs, held, sem_in, sem_out = rest[:14], rest[14:18], rest[18], rest[19]
    zl = idx[1]
    ins = [
        pltpu.make_async_copy(source, place, sem_in.at[n])
        for n, (source, place) in enumerate(zip((qkv, cot, qt, ct), held))
    ]
    for n in (3, 1, 2, 0):
        ins[n].start()
    out = []

    def leave(source, target):
        copy = pltpu.make_async_copy(source, target, sem_out.at[len(out)])
        copy.start()
        out.append(copy)

    for n in (3, 1, 2):
        ins[n].wait()
        leave(held[n].at[1 - zl], outs[7 + 2 * n])
        leave(held[n].at[zl], outs[6 + 2 * n])
    ins[0].wait()
    for k, zz, half, cols in relative_places(idx):
        leave(held[0].at[zz, :, :, cols], outs[k].at[:, :, pl.ds(256 * half, 256)])
    for copy in out:
        copy.wait()


def pack(idx, qkv, cot, qt, ct):
    outs = [shape_of(3, BLK, 512)] * 8
    outs += [shape_of(BLK, 3072)] * 2 + [shape_of(3, TXT, 256)] * 2 + [shape_of(TXT, 384)] * 2
    return pl.pallas_call(
        pack_kernel,
        out_shape=outs,
        in_specs=[SMEM, ANY, ANY, ANY, ANY],
        out_specs=[ANY] * len(outs),
        scratch_shapes=[pltpu.VMEM(v.shape, BF) for v in (qkv, cot, qt, ct)]
        + [pltpu.SemaphoreType.DMA((4,)), pltpu.SemaphoreType.DMA((22,))],
        compiler_params=params(60),
        cost_estimate=cost(0, 9 * MB),
        name="pack",
    )(idx, qkv, cot, qt, ct)


def unpack_kernel(idx, *rest):
    chunks, own, other = rest[:8], rest[8], rest[9]
    out_video, out_text, video, text, sem = rest[10:]
    zl = idx[1]
    copies = []

    def enter(source, target):
        copy = pltpu.make_async_copy(source, target, sem.at[len(copies)])
        copy.start()
        copies.append(copy)

    for k, zz, half, cols in relative_places(idx):
        enter(chunks[k].at[:, :, pl.ds(256 * half, 256)], video.at[zz, :, :, cols])
    enter(own, text.at[zl])
    enter(other, text.at[1 - zl])
    for copy in copies:
        copy.wait()
    copies = [
        pltpu.make_async_copy(video, out_video, sem.at[0]),
        pltpu.make_async_copy(text, out_text, sem.at[1]),
    ]
    for copy in copies:
        copy.start()
    for copy in copies:
        copy.wait()


def unpack(idx, chunks, own, other):
    outs = [shape_of(2, 3, BLK, 2048), shape_of(2, 3, TXT, 256)]
    return pl.pallas_call(
        unpack_kernel,
        out_shape=outs,
        in_specs=[SMEM] + [ANY] * 10,
        out_specs=[ANY] * 2,
        scratch_shapes=[pltpu.VMEM(v.shape, BF) for v in outs]
        + [pltpu.SemaphoreType.DMA((18,))],
        compiler_params=params(60),
        cost_estimate=cost(0, 6 * MB),
        name="unpack",
    )(idx, *chunks, own, other)


def join_text_kernel(idx, *rest):
    chunks, out, held, sem = rest[:8], rest[8], rest[9], rest[10]
    y, zl = idx[0], idx[1]
    copies = []
    for k, (dy, dz) in enumerate(RELS):
        s = lax.rem(y + 4 - dy, 4) * 2 + lax.rem(zl + dz, 2)
        cols = pl.ds(pl.multiple_of(s * 384, 384), 384)
        copies.append(pltpu.make_async_copy(chunks[k], held.at[:, cols], sem.at[k]))
    for copy in copies:
        copy.start()
    for copy in copies:
        copy.wait()
    copy = pltpu.make_async_copy(held, out, sem.at[0])
    copy.start()
    copy.wait()


def join_text(idx, chunks):
    return pl.pallas_call(
        join_text_kernel,
        out_shape=shape_of(TXT, 3072),
        in_specs=[SMEM] + [ANY] * 8,
        out_specs=ANY,
        scratch_shapes=[pltpu.VMEM((TXT, 3072), BF), pltpu.SemaphoreType.DMA((8,))],
        compiler_params=params(60),
        cost_estimate=cost(0, 2 * MB),
        name="join_text",
    )(idx, *chunks)


def normed_rows(raw, gain):
    wide = raw.astype(F32)
    inverse = lax.rsqrt(jnp.mean(wide * wide, axis=-1, keepdims=True) + 1e-6)
    unit = wide * inverse
    return unit, inverse, (unit * gain).astype(BF)


def joint_rows(chunks, text, part):
    return jnp.concatenate([c[part] for c in chunks], axis=0), text[part]


def dot(a, b, dims):
    return lax.dot_general(a, b, (dims, ((), ())), preferred_element_type=F32)


NN = ((1,), (0,))
NT = ((1,), (1,))
TN = ((0,), (0,))


def forward_kernel(length, gains, *rest):
    chunks, own, other = rest[:8], rest[8], rest[9]
    prob_out, att_video, att_text = rest[10:]
    text = jnp.where(pl.program_id(0) < 2, own[...], other[...])
    normed = []
    for part in range(2):
        video_raw, text_raw = joint_rows(chunks, text, part)
        normed.append(
            jnp.concatenate(
                [
                    normed_rows(video_raw, gains[0, part : part + 1])[2],
                    normed_rows(text_raw, gains[1, part : part + 1])[2],
                ],
                axis=0,
            )
        )
    values = jnp.concatenate(joint_rows(chunks, text, 2), axis=0)
    scores = dot(normed[0], normed[1], NT) * SCALE
    seen = lax.broadcasted_iota(jnp.int32, (SEQ, TXT), 1) < length[0]
    scores = jnp.concatenate(
        [scores[:, :VID], jnp.where(seen, scores[:, VID:], -1e30)], axis=1
    )
    powers = jnp.exp(scores - jnp.max(scores, axis=-1, keepdims=True))
    prob = powers * (1.0 / jnp.sum(powers, axis=-1, keepdims=True))
    prob_out[0] = prob
    attended = dot(prob.astype(BF), values, NN).astype(BF)
    att_video[...] = attended[:VID]
    att_text[...] = attended[VID:]


CHUNK = pl.BlockSpec((3, BLK, DH), lambda h: (0, 0, h))
FIRST = pl.BlockSpec((3, TXT, DH), lambda h: (0, 0, jnp.minimum(h, 1)))
LATER = pl.BlockSpec((3, TXT, DH), lambda h: (0, 0, jnp.maximum(h - 2, 0)))
GAINS = pl.BlockSpec((2, 2, DH), lambda h: (0, 0, 0))
PROB = pl.BlockSpec((1, SEQ, SEQ), lambda h: (h, 0, 0))


def forward(length, gains, chunks, own, other):
    return pl.pallas_call(
        forward_kernel,
        grid=(4,),
        out_shape=[shape_of(4, SEQ, SEQ, dtype=F32), shape_of(VID, 512), shape_of(TXT, 512)],
        in_specs=[SMEM, GAINS] + [CHUNK] * 8 + [FIRST, LATER],
        out_specs=[
            PROB,
            pl.BlockSpec((VID, DH), lambda h: (0, h)),
            pl.BlockSpec((TXT, DH), lambda h: (0, h)),
        ],
        compiler_params=params(60),
        cost_estimate=cost(4 * 4 * SEQ * SEQ * DH, 18 * MB, 4 * SEQ * SEQ),
        name="forward",
    )(length, gains, *chunks, own, other)


def norm_back(unit, inverse, gain, incoming):
    scaled = incoming * gain
    return inverse * (scaled - unit * jnp.mean(scaled * unit, axis=-1, keepdims=True))


def backward_kernel(gains, prob_ref, grad_out, *rest):
    chunks, own, other = rest[:8], rest[8], rest[9]
    outs, out_own, out_other = rest[10:18], rest[18], rest[19]
    head = pl.program_id(0)
    text = jnp.where(head < 2, own[...], other[...])
    units = []
    normed = []
    for part in range(2):
        video_raw, text_raw = joint_rows(chunks, text, part)
        v = normed_rows(video_raw, gains[0, part : part + 1])
        t = normed_rows(text_raw, gains[1, part : part + 1])
        units.append((v, t))
        normed.append(jnp.concatenate([v[2], t[2]], axis=0))
    values = jnp.concatenate(joint_rows(chunks, text, 2), axis=0)
    prob = prob_ref[0]
    rows = grad_out[...]
    grad_prob = dot(rows, values, NT)
    inner = jnp.sum(prob * grad_prob, axis=-1, keepdims=True)
    low = (prob * (grad_prob - inner) * SCALE).astype(BF)
    grad_q = dot(low, normed[1], NN)
    grad_k = dot(normed[0], low, TN).T
    grad_v = dot(rows, prob.astype(BF), TN).T
    results = []
    for part, grad in enumerate((grad_q, grad_k)):
        v, t = units[part]
        results.append(
            (
                norm_back(v[0], v[1], gains[0, part : part + 1], grad[:VID]).astype(BF),
                norm_back(t[0], t[1], gains[1, part : part + 1], grad[VID:]).astype(BF),
            )
        )
    results.append((grad_v[:VID].astype(BF), grad_v[VID:].astype(BF)))
    for part in range(3):
        for k in range(8):
            outs[k][part] = results[part][0][k * BLK : (k + 1) * BLK]

    @pl.when(head < 2)
    def _():
        for part in range(3):
            out_own[part] = results[part][1]

    @pl.when(head >= 2)
    def _():
        for part in range(3):
            out_other[part] = results[part][1]


def backward(gains, prob, grad_out, chunks, own, other):
    return pl.pallas_call(
        backward_kernel,
        grid=(4,),
        out_shape=[shape_of(3, BLK, 512)] * 8 + [shape_of(3, TXT, 256)] * 2,
        in_specs=[GAINS, PROB, pl.BlockSpec((SEQ, DH), lambda h: (0, h))]
        + [CHUNK] * 8
        + [FIRST, LATER],
        out_specs=[CHUNK] * 8 + [FIRST, LATER],
        compiler_params=params(60),
        cost_estimate=cost(4 * 8 * SEQ * SEQ * DH, 20 * MB),
        name="backward",
    )(gains, prob, grad_out, *chunks, own, other)


def grad_out_kernel(*refs):
    cots, cot_text, w_video, w_text, out, acc = refs[:8], *refs[8:]
    step = pl.program_id(0)
    video = jnp.concatenate([c[...] for c in cots], axis=0)
    text = cot_text[...]
    for half in range(2):
        cols = slice(256 * half, 256 * half + 256)
        part_v = dot(video, w_video[:, half].reshape(768, 256), NN)
        part_t = dot(text, w_text[:, half].reshape(768, 256), NN)

        @pl.when(step == 0)
        def _():
            acc[:VID, cols] = part_v
            acc[VID:, cols] = part_t

        @pl.when(step > 0)
        def _():
            acc[:VID, cols] += part_v
            acc[VID:, cols] += part_t

    @pl.when(step == 3)
    def _():
        out[...] = acc[...].astype(BF)


def project_back(cots, cot_text, weights):
    def weight_spec(stream):
        return pl.BlockSpec((8, 2, None, BLK, 256), lambda i: (i, 0, stream, 0, 0))

    return pl.pallas_call(
        grad_out_kernel,
        grid=(4,),
        out_shape=shape_of(SEQ, 512),
        in_specs=[pl.BlockSpec((BLK, 768), lambda i: (0, i))] * 8
        + [pl.BlockSpec((TXT, 768), lambda i: (0, i)), weight_spec(0), weight_spec(1)],
        out_specs=pl.BlockSpec((SEQ, 512), lambda i: (0, 0)),
        scratch_shapes=[pltpu.VMEM((SEQ, 512), F32)],
        compiler_params=params(60),
        cost_estimate=cost(2 * SEQ * 512 * 3072, 13 * MB),
        name="project_back",
    )(*cots, cot_text, weights, weights)


def weight_grad_kernel(idx, att, *refs):
    cots, keep, send = refs[:-2], refs[-2], refs[-1]
    cot = jnp.concatenate([c[...] for c in cots], axis=0) if len(cots) > 1 else cots[0][...]
    part = dot(cot, att[...], TN).reshape(2, 2, BLK, 512)
    first = idx[2] == 0
    keep[...] = jnp.where(first, part[:, 0], part[:, 1]).astype(BF)
    send[...] = jnp.where(first, part[:, 1], part[:, 0]).astype(BF)


def weight_grad(idx, att, cots, name):
    rows, per = att.shape[0], cots[0].shape[0]
    out = pl.BlockSpec((2, BLK, 512), lambda i: (i, 0, 0))
    return pl.pallas_call(
        weight_grad_kernel,
        grid=(8,),
        out_shape=[shape_of(16, BLK, 512)] * 2,
        in_specs=[SMEM, pl.BlockSpec((rows, 512), lambda i: (0, 0))]
        + [pl.BlockSpec((per, 384), lambda i: (0, i))] * len(cots),
        out_specs=[out, out],
        compiler_params=params(60),
        cost_estimate=cost(2 * rows * 512 * 3072, 8 * MB),
        name=name,
    )(idx, att, *cots)


def wide_sum(parts):
    return functools.reduce(jnp.add, [p.astype(F32) for p in parts])


def reduce_weight(idx, keep, send):
    zh, x = idx[3], idx[4]
    got = send_dp(send, 0, 0, 1)
    keep = keep.reshape(4, 4, BLK, 512)
    got = got.reshape(4, 4, BLK, 512)

    def share(step):
        at = lax.rem(x + step, 4)
        return wide_sum(
            [lax.dynamic_index_in_dim(v, at, axis=1, keepdims=False) for v in (keep, got)]
        )

    arrived = [send_dp(share(step).astype(BF), 0, step, 0) for step in (2, 1, 3)]
    total = wide_sum([share(0)] + arrived).astype(BF)

    def slab(step):
        return lax.dynamic_index_in_dim(total, lax.rem(zh + step, 4), axis=0, keepdims=False)

    arrived = [send_dp(slab(step), step, 0, 0) for step in (2, 1, 3)]
    total = wide_sum([slab(0)] + arrived)
    last = send_sp(total[:, 256:].astype(BF), 0, 1)
    return wide_sum([total[:, :256], last]).T


def body(qkv_video, qkv_text, qk_gains, text_len, w_out_video, w_out_text, cot_video, cot_text):
    sp, dp = lax.axis_index("sp"), lax.axis_index("dp")
    y, zl = sp // 2, sp % 2
    idx = jnp.stack([y, zl, dp % 2, dp // 8, (dp // 2) % 4]).astype(jnp.int32)
    length = lax.dynamic_slice(text_len, (zl,), (1,))

    packed = pack(idx, qkv_video, cot_video, qkv_text, cot_text)
    sent = packed[:8]
    cot_own, cot_send, text_own, text_send, ct_own, ct_send = packed[8:]

    w_own = jnp.stack([w_out_video.T, w_out_text.T])
    w_pair = jnp.stack([w_own, send_sp(w_own, 0, 1)])
    weights = lax.all_gather(w_pair, "dp", axis=0)

    text_other = send_sp(text_send, 0, 1)
    ct_pair = jnp.stack([ct_own, send_sp(ct_send, 0, 1)])
    ct_all = [ct_pair] + [send_sp(ct_pair, dy, 0) for dy in range(1, 4)]
    text_cot = join_text(idx, [c[n] for c in ct_all for n in range(2)])

    chunks = [sent[0]] + [send_sp(sent[k], *RELS[k]) for k in range(1, 8)]

    near = [cot_own, send_sp(cot_send, 0, 1)]
    below = [send_sp(c, 1, 0) for c in near]
    above = [send_sp(c, 3, 0) for c in near]

    prob, att_video, att_text = forward(length, qk_gains, chunks, text_own, text_other)
    text_parts = weight_grad(idx, att_text, [text_cot], "weight_text")
    passed = lax.optimization_barrier((below[0], above[1], att_video, text_parts))
    att_video, text_parts = passed[2], passed[3]
    far = [send_sp(passed[0], 1, 0), send_sp(passed[1], 3, 0)]
    cots = near + below + far + above

    grad_w_text = reduce_weight(idx, *text_parts)
    video_parts = weight_grad(idx, att_video, cots, "weight_video")
    text_cot, video_parts = lax.optimization_barrier((text_cot, video_parts))
    grad_w_video = reduce_weight(idx, *video_parts)
    grad_out = project_back(cots, text_cot, weights)
    grads = backward(qk_gains, prob, grad_out, chunks, text_own, text_other)
    back = [grads[0]] + [
        send_sp(grads[k], -RELS[k][0], RELS[k][1]) for k in range(1, 8)
    ]
    grad_qkv_video, grad_qkv_text = unpack(idx, back, grads[8], send_sp(grads[9], 0, 1))
    return (grad_qkv_video, grad_qkv_text, grad_w_video, grad_w_text)


def solution(mesh):
    return jax.shard_map(
        body,
        mesh=mesh,
        in_specs=(
            P("dp", None, "sp", None),
            P("dp", None, None, "sp"),
            P(),
            P("dp"),
            P("sp", "dp"),
            P("sp", "dp"),
            P("dp", "sp", None),
            P("dp", None, "sp"),
        ),
        out_specs=(
            P("dp", None, "sp", None),
            P("dp", None, None, "sp"),
            P("sp", "dp"),
            P("sp", "dp"),
        ),
        check_vma=False,
    )
```

```python
import functools

import jax
import jax.numpy as jnp
from jax import lax
from jax.experimental import pallas as pl
from jax.experimental.pallas import tpu as pltpu
from jax.sharding import PartitionSpec as P

DH = 128
VID = 768
TXT = 128
SEQ = VID + TXT
BLK = 96
BF = jnp.bfloat16
F32 = jnp.float32
SCALE = DH ** (-0.5)
RELS = [(dy, dz) for dy in range(4) for dz in range(2)]
ANY = pl.BlockSpec(memory_space=pl.ANY)
SMEM = pl.BlockSpec(memory_space=pltpu.SMEM)
MB = 1024 * 1024


def shape_of(*dims, dtype=BF):
    return jax.ShapeDtypeStruct(dims, dtype)


def params(mb):
    return pltpu.CompilerParams(vmem_limit_bytes=mb * MB)


def cost(flops, nbytes, exps=0):
    return pl.CostEstimate(
        flops=flops // 1000, bytes_accessed=nbytes // 1000, transcendentals=exps // 1000
    )


def sp_perm(dy, dz):
    return [(y * 2 + z, ((y + dy) % 4) * 2 + (z + dz) % 2) for y in range(4) for z in range(2)]


def send_sp(value, dy, dz):
    return lax.ppermute(value, "sp", sp_perm(dy, dz))


def dp_perm(dh, dx, dc):
    return [
        ((h * 4 + x) * 2 + c, (((h + dh) % 4) * 4 + (x + dx) % 4) * 2 + (c + dc) % 2)
        for h in range(4)
        for x in range(4)
        for c in range(2)
    ]


def send_dp(value, dh, dx, dc):
    return lax.ppermute(value, "dp", dp_perm(dh, dx, dc))


def place_of(idx, k):
    dy, dz = RELS[k]
    return lax.rem(idx[0] + 4 - dy, 4) * 2 + lax.rem(idx[1] + dz, 2)


def head_pieces():
    for s in range(8):
        y, z = s // 2, s % 2
        for half in range(2):
            yield s, z, half, pl.ds(y * 512 + (z + half) % 2 * 256, 256)


def fold_text(wide):
    tail = [wide[BLK:, n * 128 : n * 128 + 128] for n in range(3)]
    return jnp.concatenate([wide[:BLK], jnp.concatenate(tail, axis=0)], axis=1)


def unfold_text(slab):
    tail = [slab[32 * n : 32 * n + 32, 384:] for n in range(3)]
    return jnp.concatenate([slab[:, :384], jnp.concatenate(tail, axis=1)], axis=0)


def pack_kernel(idx, qkv, qt, ct, *rest):
    out, own, other, held_qkv, held_qt, held_ct, slabs, sem_in, sem_out = rest
    zl = idx[1]
    ins = [
        pltpu.make_async_copy(source, place, sem_in.at[n])
        for n, (source, place) in enumerate(((ct, held_ct), (qt, held_qt), (qkv, held_qkv)))
    ]
    for copy in ins:
        copy.start()
    outs = []

    def leave(source, target):
        copy = pltpu.make_async_copy(source, target, sem_out.at[len(outs)])
        copy.start()
        outs.append(copy)

    ins[0].wait()
    for clip in range(2):
        slabs[clip] = fold_text(held_ct[clip])
    for s in range(8):
        leave(slabs.at[s % 2], out.at[s, 3])
    ins[1].wait()
    leave(held_qt.at[zl], own)
    leave(held_qt.at[1 - zl], other)
    ins[2].wait()
    for s, clip, half, cols in head_pieces():
        leave(
            held_qkv.at[clip, :, :, cols],
            out.at[s, pl.ds(0, 3), :, pl.ds(256 * half, 256)],
        )
    for copy in outs:
        copy.wait()


def pack(idx, qkv, qt, ct):
    return pl.pallas_call(
        pack_kernel,
        out_shape=[shape_of(8, 4, BLK, 512)] + [shape_of(3, TXT, 256)] * 2,
        in_specs=[SMEM, ANY, ANY, ANY],
        out_specs=[ANY] * 3,
        scratch_shapes=[pltpu.VMEM(v.shape, BF) for v in (qkv, qt, ct)]
        + [pltpu.VMEM((2, BLK, 512), BF)]
        + [pltpu.SemaphoreType.DMA((3,)), pltpu.SemaphoreType.DMA((26,))],
        compiler_params=params(60),
        cost_estimate=cost(0, 8 * MB),
        name="pack",
    )(idx, qkv, qt, ct)


def unpack_kernel(idx, chunks, own, other, *rest):
    out_video, out_text, video, text, sem = rest
    zl = idx[1]
    copies = []

    def enter(source, target):
        copy = pltpu.make_async_copy(source, target, sem.at[len(copies)])
        copy.start()
        copies.append(copy)

    for s, clip, half, cols in head_pieces():
        enter(chunks.at[s, :, :, pl.ds(256 * half, 256)], video.at[clip, :, :, cols])
    enter(own, text.at[zl])
    enter(other, text.at[1 - zl])
    for copy in copies:
        copy.wait()
    copies = [
        pltpu.make_async_copy(video, out_video, sem.at[0]),
        pltpu.make_async_copy(text, out_text, sem.at[1]),
    ]
    for copy in copies:
        copy.start()
    for copy in copies:
        copy.wait()


def unpack(idx, chunks, own, other):
    outs = [shape_of(2, 3, BLK, 2048), shape_of(2, 3, TXT, 256)]
    return pl.pallas_call(
        unpack_kernel,
        out_shape=outs,
        in_specs=[SMEM, ANY, ANY, ANY],
        out_specs=[ANY] * 2,
        scratch_shapes=[pltpu.VMEM(v.shape, BF) for v in outs]
        + [pltpu.SemaphoreType.DMA((18,))],
        compiler_params=params(60),
        cost_estimate=cost(0, 6 * MB),
        name="unpack",
    )(idx, chunks, own, other)


def normed_rows(raw, gain):
    wide = raw.astype(F32)
    inverse = lax.rsqrt(jnp.mean(wide * wide, axis=-1, keepdims=True) + 1e-6)
    unit = wide * inverse
    return unit, inverse, (unit * gain).astype(BF)


def joint_rows(idx, chunks, text, part):
    return jnp.concatenate([chunks[place_of(idx, k), part] for k in range(8)], axis=0), text[part]


def dot(a, b, dims):
    return lax.dot_general(a, b, (dims, ((), ())), preferred_element_type=F32)


NN = ((1,), (0,))
NT = ((1,), (1,))
TN = ((0,), (0,))


def forward_kernel(idx, length, gains, chunks, own, other, prob_out, att_video, att_text):
    text = jnp.where(pl.program_id(0) < 2, own[...], other[...])
    normed = []
    for part in range(2):
        video_raw, text_raw = joint_rows(idx, chunks, text, part)
        normed.append(
            jnp.concatenate(
                [
                    normed_rows(video_raw, gains[0, part : part + 1])[2],
                    normed_rows(text_raw, gains[1, part : part + 1])[2],
                ],
                axis=0,
            )
        )
    values = jnp.concatenate(joint_rows(idx, chunks, text, 2), axis=0)
    scores = dot(normed[0], normed[1], NT) * SCALE
    seen = lax.broadcasted_iota(jnp.int32, (SEQ, TXT), 1) < length[0]
    scores = jnp.concatenate(
        [scores[:, :VID], jnp.where(seen, scores[:, VID:], -1e30)], axis=1
    )
    powers = jnp.exp(scores - jnp.max(scores, axis=-1, keepdims=True))
    prob = powers * (1.0 / jnp.sum(powers, axis=-1, keepdims=True))
    prob_out[0] = prob
    attended = dot(prob.astype(BF), values, NN).astype(BF)
    att_video[...] = attended[:VID]
    att_text[...] = attended[VID:]


CHUNK = pl.BlockSpec((8, 3, BLK, DH), lambda h: (0, 0, 0, h))
FIRST = pl.BlockSpec((3, TXT, DH), lambda h: (0, 0, jnp.minimum(h, 1)))
LATER = pl.BlockSpec((3, TXT, DH), lambda h: (0, 0, jnp.maximum(h - 2, 0)))
GAINS = pl.BlockSpec((2, 2, DH), lambda h: (0, 0, 0))
PROB = pl.BlockSpec((1, SEQ, SEQ), lambda h: (h, 0, 0))


def forward(idx, length, gains, chunks, own, other):
    return pl.pallas_call(
        forward_kernel,
        grid=(4,),
        out_shape=[shape_of(4, SEQ, SEQ, dtype=F32), shape_of(VID, 512), shape_of(TXT, 512)],
        in_specs=[SMEM, SMEM, GAINS, CHUNK, FIRST, LATER],
        out_specs=[
            PROB,
            pl.BlockSpec((VID, DH), lambda h: (0, h)),
            pl.BlockSpec((TXT, DH), lambda h: (0, h)),
        ],
        compiler_params=params(60),
        cost_estimate=cost(4 * 4 * SEQ * SEQ * DH, 18 * MB, 4 * SEQ * SEQ),
        name="forward",
    )(idx, length, gains, chunks, own, other)


def norm_back(unit, inverse, gain, incoming):
    scaled = incoming * gain
    return inverse * (scaled - unit * jnp.mean(scaled * unit, axis=-1, keepdims=True))


def backward_kernel(
    idx, gains, prob_ref, grad_out, chunks, own, other, outs, out_own, out_other
):
    head = pl.program_id(0)
    text = jnp.where(head < 2, own[...], other[...])
    units = []
    normed = []
    for part in range(2):
        video_raw, text_raw = joint_rows(idx, chunks, text, part)
        v = normed_rows(video_raw, gains[0, part : part + 1])
        t = normed_rows(text_raw, gains[1, part : part + 1])
        units.append((v, t))
        normed.append(jnp.concatenate([v[2], t[2]], axis=0))
    values = jnp.concatenate(joint_rows(idx, chunks, text, 2), axis=0)
    prob = prob_ref[0]
    rows = grad_out[...]
    grad_prob = dot(rows, values, NT)
    inner = jnp.sum(prob * grad_prob, axis=-1, keepdims=True)
    low = (prob * (grad_prob - inner) * SCALE).astype(BF)
    grad_q = dot(low, normed[1], NN)
    grad_k = dot(normed[0], low, TN).T
    grad_v = dot(rows, prob.astype(BF), TN).T
    results = []
    for part, grad in enumerate((grad_q, grad_k)):
        v, t = units[part]
        results.append(
            (
                norm_back(v[0], v[1], gains[0, part : part + 1], grad[:VID]).astype(BF),
                norm_back(t[0], t[1], gains[1, part : part + 1], grad[VID:]).astype(BF),
            )
        )
    results.append((grad_v[:VID].astype(BF), grad_v[VID:].astype(BF)))
    for part in range(3):
        for k in range(8):
            outs[place_of(idx, k), part] = results[part][0][k * BLK : (k + 1) * BLK]

    @pl.when(head < 2)
    def _():
        for part in range(3):
            out_own[part] = results[part][1]

    @pl.when(head >= 2)
    def _():
        for part in range(3):
            out_other[part] = results[part][1]


def backward(idx, gains, prob, grad_out, chunks, own, other):
    return pl.pallas_call(
        backward_kernel,
        grid=(4,),
        out_shape=[shape_of(8, 3, BLK, 512)] + [shape_of(3, TXT, 256)] * 2,
        in_specs=[SMEM, GAINS, PROB, pl.BlockSpec((SEQ, DH), lambda h: (0, h))]
        + [CHUNK, FIRST, LATER],
        out_specs=[CHUNK, FIRST, LATER],
        compiler_params=params(60),
        cost_estimate=cost(4 * 8 * SEQ * SEQ * DH, 20 * MB),
        name="backward",
    )(idx, gains, prob, grad_out, chunks, own, other)


def grad_out_kernel(idx, *refs):
    cots, cot_text, mine, theirs, out, acc = refs[:8], *refs[8:]
    step = pl.program_id(0)
    video = jnp.concatenate([c[...] for c in cots], axis=0)
    text = jnp.concatenate([unfold_text(cot_text[n]) for n in range(2)], axis=1)

    def add(core_0, core_1):
        for half in range(2):
            cols = slice(256 * half, 256 * half + 256)
            for stream, rows, left in ((0, slice(0, VID), video), (1, slice(VID, SEQ), text)):
                weight = jnp.stack(
                    [core_0[:, half, stream], core_1[:, half, stream]], axis=1
                ).reshape(768, 256)
                part = dot(left, weight, NN)
                acc[rows, cols] = jnp.where(step == 0, part, acc[rows, cols] + part)

    @pl.when(idx[2] == 0)
    def _():
        add(mine, theirs)

    @pl.when(idx[2] == 1)
    def _():
        add(theirs, mine)

    @pl.when(step == 3)
    def _():
        out[...] = acc[...].astype(BF)


def project_back(idx, cots, cot_text, mine, theirs):
    weight = pl.BlockSpec((4, 2, 2, BLK, 256), lambda i: (i, 0, 0, 0, 0))
    return pl.pallas_call(
        grad_out_kernel,
        grid=(4,),
        in_specs=[SMEM]
        + [pl.BlockSpec((BLK, 768), lambda i: (0, i))] * 8
        + [pl.BlockSpec((2, None, BLK, 512), lambda i: (i, 3, 0, 0))]
        + [weight, weight],
        out_specs=pl.BlockSpec((SEQ, 512), lambda i: (0, 0)),
        scratch_shapes=[pltpu.VMEM((SEQ, 512), F32)],
        out_shape=shape_of(SEQ, 512),
        compiler_params=params(60),
        cost_estimate=cost(2 * SEQ * 512 * 3072, 13 * MB),
        name="project_back",
    )(idx, *cots, cot_text, mine, theirs)


def weight_grad_kernel(idx, att, *refs):
    cots, keep, send = refs[:-2], refs[-2], refs[-1]
    if len(cots) > 1:
        cot = jnp.concatenate([c[...] for c in cots], axis=0)
    else:
        cot = unfold_text(cots[0][...])
    part = dot(cot, att[...], TN).reshape(2, 2, BLK, 512)
    first = idx[2] == 0
    keep[...] = jnp.where(first, part[:, 0], part[:, 1]).astype(BF)
    send[...] = jnp.where(first, part[:, 1], part[:, 0]).astype(BF)


def weight_grad(idx, att, cots, name):
    rows = att.shape[0]
    out = pl.BlockSpec((2, BLK, 512), lambda i: (i, 0, 0))
    if len(cots) > 1:
        specs = [pl.BlockSpec((BLK, 384), lambda i: (0, i))] * len(cots)
    else:
        specs = [pl.BlockSpec((None, None, BLK, 512), lambda i: (i, 3, 0, 0))]
    return pl.pallas_call(
        weight_grad_kernel,
        grid=(8,),
        out_shape=[shape_of(16, BLK, 512)] * 2,
        in_specs=[SMEM, pl.BlockSpec((rows, 512), lambda i: (0, 0))] + specs,
        out_specs=[out, out],
        compiler_params=params(60),
        cost_estimate=cost(2 * rows * 512 * 3072, 8 * MB),
        name=name,
    )(idx, att, *cots)


def wide_sum(parts):
    return functools.reduce(jnp.add, [p.astype(F32) for p in parts])


def sum_cores(idx, keep, got):
    keep = keep.reshape(4, 4, BLK, 512)
    got = got.reshape(4, 4, BLK, 512)

    def share(step):
        at = lax.rem(idx[4] + step, 4)
        return wide_sum(
            [lax.dynamic_index_in_dim(v, at, axis=1, keepdims=False) for v in (keep, got)]
        )

    return [share(step).astype(BF) for step in range(4)]


def send_x(shares, steps):
    return [send_dp(shares[step], 0, step, 0) for step in steps]


def sum_far_and_near(idx, totals):
    zh = idx[3]

    def slab(step):
        at = lax.rem(zh + step, 4)
        return jnp.stack(
            [lax.dynamic_index_in_dim(t, at, axis=0, keepdims=False) for t in totals]
        )

    arrived = [send_dp(slab(step), step, 0, 0) for step in (2, 1, 3)]
    total = wide_sum([slab(0)] + arrived)
    last = send_sp(total[:, :, 256:].astype(BF), 0, 1)
    total = wide_sum([total[:, :, :256], last])
    return [total[n].T for n in range(2)]


def body(qkv_video, qkv_text, qk_gains, text_len, w_out_video, w_out_text, cot_video, cot_text):
    sp, dp = lax.axis_index("sp"), lax.axis_index("dp")
    y, zl = sp // 2, sp % 2
    idx = jnp.stack([y, zl, dp % 2, dp // 8, (dp // 2) % 4]).astype(jnp.int32)
    length = lax.dynamic_slice(text_len, (zl,), (1,))

    after = lax.optimization_barrier

    def of_clip(array, clip):
        return lax.dynamic_index_in_dim(array, clip, axis=0, keepdims=False)

    cot_own = of_clip(cot_video, zl)
    cot_send = of_clip(cot_video, 1 - zl)
    w_own = jnp.stack([w_out_video.T, w_out_text.T])
    cot_own, cot_send, w_own = after((cot_own, cot_send, w_own))

    near = [cot_own, send_sp(cot_send, 0, 1)]
    below, above = [send_sp(cot_own, 1, 0)], [send_sp(cot_own, 3, 0)]
    w_pair = jnp.stack([w_own, send_sp(w_own, 0, 1)])
    packed = pack(idx, qkv_video, qkv_text, cot_text)
    near, below, above, packed, w_pair = after((near, below, above, packed, w_pair))

    weights = lax.all_gather(
        w_pair,
        "dp",
        axis=0,
        axis_index_groups=[[2 * n + core for n in range(16)] for core in range(2)],
    )
    below = below + [send_sp(near[1], 1, 0)]
    above = above + [send_sp(near[1], 3, 0)]
    sent, text_own, text_send = packed
    text_other = send_sp(text_send, 0, 1)
    chunks = lax.all_to_all(sent, "sp", 0, 0, tiled=True)
    below, above, chunks, text_other = after((below, above, chunks, text_other))

    far = [send_sp(below[0], 1, 0), send_sp(above[1], 3, 0)]
    prob, att_video, att_text = forward(
        idx, length, qk_gains, chunks, text_own, text_other
    )
    att_video, att_text, far = after((att_video, att_text, far))

    cots = near + below + far + above

    text_keep, text_give = weight_grad(idx, att_text, [chunks], "weight_text")
    text_keep, text_give, weights = after((text_keep, text_give, weights))

    other_weights = send_dp(weights, 0, 0, 1)
    text_got = send_dp(text_give, 0, 0, 1)
    keep, give = weight_grad(idx, att_video, cots, "weight_video")
    text_got, keep, give, other_weights = after((text_got, keep, give, other_weights))

    text_shares = sum_cores(idx, text_keep, text_got)
    text_shares, give, cots = after((text_shares, give, cots))

    text_near = send_x(text_shares, (1, 3))
    got = send_dp(give, 0, 0, 1)
    grad_out = project_back(idx, cots, chunks, weights, other_weights)
    text_near, got, keep, grad_out = after((text_near, got, keep, grad_out))

    shares = sum_cores(idx, keep, got)
    shares, text_shares, grad_out = after((shares, text_shares, grad_out))

    near_sums = send_x(shares, (1, 3))
    text_far = send_x(text_shares, (2,))
    grads, own, other = backward(
        idx, qk_gains, prob, grad_out, chunks, text_own, text_other
    )
    near_sums, text_far, grads, other, shares = after(
        (near_sums, text_far, grads, other, shares)
    )

    far_sums = send_x(shares, (2,))
    grads = lax.all_to_all(grads, "sp", 0, 0, tiled=True)
    other = send_sp(other, 0, 1)
    text_total = wide_sum([text_shares[0]] + text_near + text_far).astype(BF)
    video_total = wide_sum([shares[0]] + near_sums + far_sums).astype(BF)
    grad_w_text, grad_w_video = sum_far_and_near(idx, (text_total, video_total))
    grad_qkv_video, grad_qkv_text = unpack(idx, grads, own, other)
    return (grad_qkv_video, grad_qkv_text, grad_w_video, grad_w_text)


def solution(mesh):
    return jax.shard_map(
        body,
        mesh=mesh,
        in_specs=(
            P("dp", None, "sp", None),
            P("dp", None, None, "sp"),
            P(),
            P("dp"),
            P("sp", "dp"),
            P("sp", "dp"),
            P("dp", "sp", None),
            P("dp", None, "sp"),
        ),
        out_specs=(
            P("dp", None, "sp", None),
            P("dp", None, None, "sp"),
            P("sp", "dp"),
            P("sp", "dp"),
        ),
        check_vma=False,
    )
```

```python
import functools

import jax
import jax.numpy as jnp
from jax import lax
from jax.experimental import pallas as pl
from jax.experimental.pallas import tpu as pltpu
from jax.sharding import PartitionSpec as P

DH = 128
VID = 768
TXT = 128
SEQ = VID + TXT
BLK = 96
BF = jnp.bfloat16
F32 = jnp.float32
SCALE = DH ** (-0.5)
RELS = [(dy, dz) for dy in range(4) for dz in range(2)]
ANY = pl.BlockSpec(memory_space=pl.ANY)
SMEM = pl.BlockSpec(memory_space=pltpu.SMEM)
MB = 1024 * 1024


def shape_of(*dims, dtype=BF):
    return jax.ShapeDtypeStruct(dims, dtype)


def params(mb):
    return pltpu.CompilerParams(vmem_limit_bytes=mb * MB)


def cost(flops, nbytes, exps=0):
    return pl.CostEstimate(
        flops=flops // 1000, bytes_accessed=nbytes // 1000, transcendentals=exps // 1000
    )


def sp_perm(dy, dz):
    return [(y * 2 + z, ((y + dy) % 4) * 2 + (z + dz) % 2) for y in range(4) for z in range(2)]


def send_sp(value, dy, dz):
    return lax.ppermute(value, "sp", sp_perm(dy, dz))


def dp_perm(dh, dx, dc):
    return [
        ((h * 4 + x) * 2 + c, (((h + dh) % 4) * 4 + (x + dx) % 4) * 2 + (c + dc) % 2)
        for h in range(4)
        for x in range(4)
        for c in range(2)
    ]


def send_dp(value, dh, dx, dc):
    return lax.ppermute(value, "dp", dp_perm(dh, dx, dc))


def place_of(idx, k):
    dy, dz = RELS[k]
    return lax.rem(idx[0] + 4 - dy, 4) * 2 + lax.rem(idx[1] + dz, 2)


def head_pieces():
    for s in range(8):
        y, z = s // 2, s % 2
        for half in range(2):
            yield s, z, half, pl.ds(y * 512 + (z + half) % 2 * 256, 256)


def fold_text(wide):
    tail = [wide[BLK:, n * 128 : n * 128 + 128] for n in range(3)]
    return jnp.concatenate([wide[:BLK], jnp.concatenate(tail, axis=0)], axis=1)


def unfold_text(slab):
    tail = [slab[32 * n : 32 * n + 32, 384:] for n in range(3)]
    return jnp.concatenate([slab[:, :384], jnp.concatenate(tail, axis=1)], axis=0)


def pack_kernel(idx, qkv, qt, ct, *rest):
    out, own, other, held_qkv, held_qt, held_ct, slabs, sem_in, sem_out = rest
    zl = idx[1]
    ins = [
        pltpu.make_async_copy(source, place, sem_in.at[n])
        for n, (source, place) in enumerate(((ct, held_ct), (qt, held_qt), (qkv, held_qkv)))
    ]
    for copy in ins:
        copy.start()
    outs = []

    def leave(source, target):
        copy = pltpu.make_async_copy(source, target, sem_out.at[len(outs)])
        copy.start()
        outs.append(copy)

    ins[0].wait()
    for clip in range(2):
        slabs[clip] = fold_text(held_ct[clip])
    for s in range(8):
        leave(slabs.at[s % 2], out.at[s, 3])
    ins[1].wait()
    leave(held_qt.at[zl], own)
    leave(held_qt.at[1 - zl], other)
    ins[2].wait()
    for s, clip, half, cols in head_pieces():
        leave(
            held_qkv.at[clip, :, :, cols],
            out.at[s, pl.ds(0, 3), :, pl.ds(256 * half, 256)],
        )
    for copy in outs:
        copy.wait()


def pack(idx, qkv, qt, ct):
    return pl.pallas_call(
        pack_kernel,
        out_shape=[shape_of(8, 4, BLK, 512)] + [shape_of(3, TXT, 256)] * 2,
        in_specs=[SMEM, ANY, ANY, ANY],
        out_specs=[ANY] * 3,
        scratch_shapes=[pltpu.VMEM(v.shape, BF) for v in (qkv, qt, ct)]
        + [pltpu.VMEM((2, BLK, 512), BF)]
        + [pltpu.SemaphoreType.DMA((3,)), pltpu.SemaphoreType.DMA((26,))],
        compiler_params=params(60),
        cost_estimate=cost(0, 8 * MB),
        name="pack",
    )(idx, qkv, qt, ct)


def unpack_kernel(idx, chunks, own, other, *rest):
    out_video, out_text, video, text, sem = rest
    zl = idx[1]
    copies = []

    def enter(source, target):
        copy = pltpu.make_async_copy(source, target, sem.at[len(copies)])
        copy.start()
        copies.append(copy)

    for s, clip, half, cols in head_pieces():
        enter(chunks.at[s, :, :, pl.ds(256 * half, 256)], video.at[clip, :, :, cols])
    enter(own, text.at[zl])
    enter(other, text.at[1 - zl])
    for copy in copies:
        copy.wait()
    copies = [
        pltpu.make_async_copy(video, out_video, sem.at[0]),
        pltpu.make_async_copy(text, out_text, sem.at[1]),
    ]
    for copy in copies:
        copy.start()
    for copy in copies:
        copy.wait()


def unpack(idx, chunks, own, other):
    outs = [shape_of(2, 3, BLK, 2048), shape_of(2, 3, TXT, 256)]
    return pl.pallas_call(
        unpack_kernel,
        out_shape=outs,
        in_specs=[SMEM, ANY, ANY, ANY],
        out_specs=[ANY] * 2,
        scratch_shapes=[pltpu.VMEM(v.shape, BF) for v in outs]
        + [pltpu.SemaphoreType.DMA((18,))],
        compiler_params=params(60),
        cost_estimate=cost(0, 6 * MB),
        name="unpack",
    )(idx, chunks, own, other)


def normed_rows(raw, gain):
    wide = raw.astype(F32)
    inverse = lax.rsqrt(jnp.mean(wide * wide, axis=-1, keepdims=True) + 1e-6)
    unit = wide * inverse
    return unit, inverse, (unit * gain).astype(BF)


def joint_rows(idx, chunks, text, part):
    return jnp.concatenate([chunks[place_of(idx, k), part] for k in range(8)], axis=0), text[part]


def dot(a, b, dims):
    return lax.dot_general(a, b, (dims, ((), ())), preferred_element_type=F32)


NN = ((1,), (0,))
NT = ((1,), (1,))
TN = ((0,), (0,))


def forward_kernel(idx, length, gains, chunks, own, other, prob_out, att_video, att_text):
    text = jnp.where(pl.program_id(0) < 2, own[...], other[...])
    normed = []
    for part in range(2):
        video_raw, text_raw = joint_rows(idx, chunks, text, part)
        normed.append(
            jnp.concatenate(
                [
                    normed_rows(video_raw, gains[0, part : part + 1])[2],
                    normed_rows(text_raw, gains[1, part : part + 1])[2],
                ],
                axis=0,
            )
        )
    values = jnp.concatenate(joint_rows(idx, chunks, text, 2), axis=0)
    scores = dot(normed[0], normed[1], NT) * SCALE
    seen = lax.broadcasted_iota(jnp.int32, (SEQ, TXT), 1) < length[0]
    scores = jnp.concatenate(
        [scores[:, :VID], jnp.where(seen, scores[:, VID:], -1e30)], axis=1
    )
    powers = jnp.exp(scores - jnp.max(scores, axis=-1, keepdims=True))
    prob = powers * (1.0 / jnp.sum(powers, axis=-1, keepdims=True))
    prob_out[0] = prob
    attended = dot(prob.astype(BF), values, NN).astype(BF)
    att_video[...] = attended[:VID]
    att_text[...] = attended[VID:]


CHUNK = pl.BlockSpec((8, 3, BLK, DH), lambda h: (0, 0, 0, h))
FIRST = pl.BlockSpec((3, TXT, DH), lambda h: (0, 0, jnp.minimum(h, 1)))
LATER = pl.BlockSpec((3, TXT, DH), lambda h: (0, 0, jnp.maximum(h - 2, 0)))
GAINS = pl.BlockSpec((2, 2, DH), lambda h: (0, 0, 0))
PROB = pl.BlockSpec((1, SEQ, SEQ), lambda h: (h, 0, 0))


def forward(idx, length, gains, chunks, own, other):
    return pl.pallas_call(
        forward_kernel,
        grid=(4,),
        out_shape=[shape_of(4, SEQ, SEQ, dtype=F32), shape_of(VID, 512), shape_of(TXT, 512)],
        in_specs=[SMEM, SMEM, GAINS, CHUNK, FIRST, LATER],
        out_specs=[
            PROB,
            pl.BlockSpec((VID, DH), lambda h: (0, h)),
            pl.BlockSpec((TXT, DH), lambda h: (0, h)),
        ],
        compiler_params=params(60),
        cost_estimate=cost(4 * 4 * SEQ * SEQ * DH, 18 * MB, 4 * SEQ * SEQ),
        name="forward",
    )(idx, length, gains, chunks, own, other)


def norm_back(unit, inverse, gain, incoming):
    scaled = incoming * gain
    return inverse * (scaled - unit * jnp.mean(scaled * unit, axis=-1, keepdims=True))


def backward_kernel(
    idx, gains, prob_ref, grad_out, chunks, own, other, outs, out_own, out_other
):
    head = pl.program_id(0)
    text = jnp.where(head < 2, own[...], other[...])
    units = []
    normed = []
    for part in range(2):
        video_raw, text_raw = joint_rows(idx, chunks, text, part)
        v = normed_rows(video_raw, gains[0, part : part + 1])
        t = normed_rows(text_raw, gains[1, part : part + 1])
        units.append((v, t))
        normed.append(jnp.concatenate([v[2], t[2]], axis=0))
    values = jnp.concatenate(joint_rows(idx, chunks, text, 2), axis=0)
    prob = prob_ref[0]
    rows = grad_out[...]
    grad_prob = dot(rows, values, NT)
    inner = jnp.sum(prob * grad_prob, axis=-1, keepdims=True)
    low = (prob * (grad_prob - inner) * SCALE).astype(BF)
    grad_q = dot(low, normed[1], NN)
    grad_k = dot(normed[0], low, TN).T
    grad_v = dot(rows, prob.astype(BF), TN).T
    results = []
    for part, grad in enumerate((grad_q, grad_k)):
        v, t = units[part]
        results.append(
            (
                norm_back(v[0], v[1], gains[0, part : part + 1], grad[:VID]).astype(BF),
                norm_back(t[0], t[1], gains[1, part : part + 1], grad[VID:]).astype(BF),
            )
        )
    results.append((grad_v[:VID].astype(BF), grad_v[VID:].astype(BF)))
    for part in range(3):
        for k in range(8):
            outs[place_of(idx, k), part] = results[part][0][k * BLK : (k + 1) * BLK]

    @pl.when(head < 2)
    def _():
        for part in range(3):
            out_own[part] = results[part][1]

    @pl.when(head >= 2)
    def _():
        for part in range(3):
            out_other[part] = results[part][1]


def backward(idx, gains, prob, grad_out, chunks, own, other):
    return pl.pallas_call(
        backward_kernel,
        grid=(4,),
        out_shape=[shape_of(8, 3, BLK, 512)] + [shape_of(3, TXT, 256)] * 2,
        in_specs=[SMEM, GAINS, PROB, pl.BlockSpec((SEQ, DH), lambda h: (0, h))]
        + [CHUNK, FIRST, LATER],
        out_specs=[CHUNK, FIRST, LATER],
        compiler_params=params(60),
        cost_estimate=cost(4 * 8 * SEQ * SEQ * DH, 20 * MB),
        name="backward",
    )(idx, gains, prob, grad_out, chunks, own, other)


def grad_out_kernel(idx, *refs):
    cots, cot_text, mine, theirs, out, acc = refs[:8], *refs[8:]
    step = pl.program_id(0)
    video = jnp.concatenate([c[...] for c in cots], axis=0)
    text = jnp.concatenate([unfold_text(cot_text[n]) for n in range(2)], axis=1)

    def add(core_0, core_1):
        for half in range(2):
            cols = slice(256 * half, 256 * half + 256)
            for stream, rows, left in ((0, slice(0, VID), video), (1, slice(VID, SEQ), text)):
                weight = jnp.stack(
                    [core_0[:, half, stream], core_1[:, half, stream]], axis=1
                ).reshape(768, 256)
                part = dot(left, weight, NN)
                acc[rows, cols] = jnp.where(step == 0, part, acc[rows, cols] + part)

    @pl.when(idx[2] == 0)
    def _():
        add(mine, theirs)

    @pl.when(idx[2] == 1)
    def _():
        add(theirs, mine)

    @pl.when(step == 3)
    def _():
        out[...] = acc[...].astype(BF)


def project_back(idx, cots, cot_text, mine, theirs):
    weight = pl.BlockSpec((4, 2, 2, BLK, 256), lambda i: (i, 0, 0, 0, 0))
    return pl.pallas_call(
        grad_out_kernel,
        grid=(4,),
        in_specs=[SMEM]
        + [pl.BlockSpec((BLK, 768), lambda i: (0, i))] * 8
        + [pl.BlockSpec((2, None, BLK, 512), lambda i: (i, 3, 0, 0))]
        + [weight, weight],
        out_specs=pl.BlockSpec((SEQ, 512), lambda i: (0, 0)),
        scratch_shapes=[pltpu.VMEM((SEQ, 512), F32)],
        out_shape=shape_of(SEQ, 512),
        compiler_params=params(60),
        cost_estimate=cost(2 * SEQ * 512 * 3072, 13 * MB),
        name="project_back",
    )(idx, *cots, cot_text, mine, theirs)


def weight_grad_kernel(idx, att_video, att_text, cot_text, *refs):
    cots, keep, give = refs[:8], refs[8], refs[9]
    video = jnp.concatenate([c[...] for c in cots], axis=0)
    first = idx[2] == 0
    for stream, (cot, att) in enumerate(
        ((video, att_video), (unfold_text(cot_text[...]), att_text))
    ):
        part = dot(cot, att[...], TN).reshape(2, 2, BLK, 512)
        keep[stream] = jnp.where(first, part[:, 0], part[:, 1]).astype(BF)
        give[stream] = jnp.where(first, part[:, 1], part[:, 0]).astype(BF)


def weight_grad(idx, att_video, att_text, chunks, cots):
    def whole(rows):
        return pl.BlockSpec((rows, 512), lambda i: (0, 0))

    return pl.pallas_call(
        weight_grad_kernel,
        grid=(8,),
        out_shape=[shape_of(2, 16, BLK, 512)] * 2,
        in_specs=[SMEM, whole(VID), whole(TXT)]
        + [pl.BlockSpec((None, None, BLK, 512), lambda i: (i, 3, 0, 0))]
        + [pl.BlockSpec((BLK, 384), lambda i: (0, i))] * 8,
        out_specs=[pl.BlockSpec((2, 2, BLK, 512), lambda i: (0, i, 0, 0))] * 2,
        compiler_params=params(60),
        cost_estimate=cost(2 * SEQ * 512 * 3072, 12 * MB),
        name="weight_grad",
    )(idx, att_video, att_text, chunks, *cots)


def wide_sum(parts):
    return functools.reduce(jnp.add, [p.astype(F32) for p in parts])


def sum_cores(idx, keep, got):
    keep = keep.reshape(2, 4, 4, BLK, 512)
    got = got.reshape(2, 4, 4, BLK, 512)

    def share(step):
        at = lax.rem(idx[4] + step, 4)
        return wide_sum(
            [lax.dynamic_index_in_dim(v, at, axis=2, keepdims=False) for v in (keep, got)]
        )

    return [share(step).astype(BF) for step in range(4)]


def send_x(shares, steps):
    return [send_dp(shares[step], 0, step, 0) for step in steps]


def sum_far_and_near(idx, total):
    def slab(step):
        return lax.dynamic_index_in_dim(
            total, lax.rem(idx[3] + step, 4), axis=1, keepdims=False
        )

    arrived = [send_dp(slab(step), step, 0, 0) for step in (2, 1, 3)]
    total = wide_sum([slab(0)] + arrived)
    last = send_sp(total[:, :, 256:].astype(BF), 0, 1)
    total = wide_sum([total[:, :, :256], last])
    return [total[n].T for n in range(2)]


def body(qkv_video, qkv_text, qk_gains, text_len, w_out_video, w_out_text, cot_video, cot_text):
    sp, dp = lax.axis_index("sp"), lax.axis_index("dp")
    y, zl = sp // 2, sp % 2
    idx = jnp.stack([y, zl, dp % 2, dp // 8, (dp // 2) % 4]).astype(jnp.int32)
    length = lax.dynamic_slice(text_len, (zl,), (1,))

    after = lax.optimization_barrier

    def of_clip(array, clip):
        return lax.dynamic_index_in_dim(array, clip, axis=0, keepdims=False)

    cot_own = of_clip(cot_video, zl)
    cot_send = of_clip(cot_video, 1 - zl)
    w_own = jnp.stack([w_out_video.T, w_out_text.T])
    cot_own, cot_send = after((cot_own, cot_send))

    near = [cot_own, send_sp(cot_send, 0, 1)]
    below, above = [send_sp(cot_own, 1, 0)], [send_sp(cot_own, 3, 0)]
    w_pair = jnp.stack([w_own, send_sp(w_own, 0, 1)])
    packed = pack(idx, qkv_video, qkv_text, cot_text)
    near, below, above, packed = after((near, below, above, packed))

    weights = lax.all_gather(
        w_pair,
        "dp",
        axis=0,
        axis_index_groups=[[2 * n + core for n in range(16)] for core in range(2)],
    )
    below = below + [send_sp(near[1], 1, 0)]
    above = above + [send_sp(near[1], 3, 0)]
    sent, text_own, text_send = packed
    text_other = send_sp(text_send, 0, 1)
    chunks = lax.all_to_all(sent, "sp", 0, 0, tiled=True)
    below, above, chunks, text_other = after((below, above, chunks, text_other))

    far = [send_sp(below[0], 1, 0), send_sp(above[1], 3, 0)]
    prob, att_video, att_text = forward(
        idx, length, qk_gains, chunks, text_own, text_other
    )
    att_video, att_text, far = after((att_video, att_text, far))

    cots = near + below + far + above

    keep, give = weight_grad(idx, att_video, att_text, chunks, cots)
    keep, give, weights = after((keep, give, weights))

    other_weights = send_dp(weights, 0, 0, 1)
    give, cots, other_weights = after((give, cots, other_weights))

    got = send_dp(give, 0, 0, 1)
    grad_out = project_back(idx, cots, chunks, weights, other_weights)
    got, keep, grad_out = after((got, keep, grad_out))

    shares = sum_cores(idx, keep, got)
    shares, grad_out = after((shares, grad_out))

    near_sums = send_x(shares, (1, 3))
    grads, own, other = backward(
        idx, qk_gains, prob, grad_out, chunks, text_own, text_other
    )
    near_sums, grads, other, shares = after((near_sums, grads, other, shares))

    far_sums = send_x(shares, (2,))
    grads = lax.all_to_all(grads, "sp", 0, 0, tiled=True)
    other = send_sp(other, 0, 1)
    total = wide_sum([shares[0]] + near_sums + far_sums).astype(BF)
    grad_w_video, grad_w_text = sum_far_and_near(idx, total)
    grad_qkv_video, grad_qkv_text = unpack(idx, grads, own, other)
    return (grad_qkv_video, grad_qkv_text, grad_w_video, grad_w_text)


def solution(mesh):
    return jax.shard_map(
        body,
        mesh=mesh,
        in_specs=(
            P("dp", None, "sp", None),
            P("dp", None, None, "sp"),
            P(),
            P("dp"),
            P("sp", "dp"),
            P("sp", "dp"),
            P("dp", "sp", None),
            P("dp", None, "sp"),
        ),
        out_specs=(
            P("dp", None, "sp", None),
            P("dp", None, None, "sp"),
            P("sp", "dp"),
            P("sp", "dp"),
        ),
        check_vma=False,
    )
```

```python
import functools

import jax
import jax.numpy as jnp
from jax import lax
from jax.experimental import pallas as pl
from jax.experimental.pallas import tpu as pltpu
from jax.sharding import PartitionSpec as P

DH = 128
VID = 768
TXT = 128
SEQ = VID + TXT
BLK = 96
BF = jnp.bfloat16
F32 = jnp.float32
SCALE = DH ** (-0.5)
RELS = [(dy, dz) for dy in range(4) for dz in range(2)]
ANY = pl.BlockSpec(memory_space=pl.ANY)
SMEM = pl.BlockSpec(memory_space=pltpu.SMEM)
MB = 1024 * 1024


def shape_of(*dims, dtype=BF):
    return jax.ShapeDtypeStruct(dims, dtype)


def params(mb):
    return pltpu.CompilerParams(vmem_limit_bytes=mb * MB)


def cost(flops, nbytes, exps=0):
    return pl.CostEstimate(
        flops=flops // 1000, bytes_accessed=nbytes // 1000, transcendentals=exps // 1000
    )


def sp_perm(dy, dz):
    return [(y * 2 + z, ((y + dy) % 4) * 2 + (z + dz) % 2) for y in range(4) for z in range(2)]


def send_sp(value, dy, dz):
    return lax.ppermute(value, "sp", sp_perm(dy, dz))


def dp_perm(dh, dx, dc):
    return [
        ((h * 4 + x) * 2 + c, (((h + dh) % 4) * 4 + (x + dx) % 4) * 2 + (c + dc) % 2)
        for h in range(4)
        for x in range(4)
        for c in range(2)
    ]


def send_dp(value, dh, dx, dc):
    return lax.ppermute(value, "dp", dp_perm(dh, dx, dc))


def place_of(idx, k):
    dy, dz = RELS[k]
    return lax.rem(idx[0] + 4 - dy, 4) * 2 + lax.rem(idx[1] + dz, 2)


def head_pieces():
    for s in range(8):
        y, z = s // 2, s % 2
        for half in range(2):
            yield s, z, half, pl.ds(y * 512 + (z + half) % 2 * 256, 256)


def fold_text(wide):
    tail = [wide[BLK:, n * 128 : n * 128 + 128] for n in range(3)]
    return jnp.concatenate([wide[:BLK], jnp.concatenate(tail, axis=0)], axis=1)


def unfold_text(slab):
    tail = [slab[32 * n : 32 * n + 32, 384:] for n in range(3)]
    return jnp.concatenate([slab[:, :384], jnp.concatenate(tail, axis=1)], axis=0)


def pack_kernel(idx, qkv, qt, ct, *rest):
    out, own, other, held_qkv, held_qt, held_ct, slabs, sem_in, sem_out = rest
    zl = idx[1]
    ins = [
        pltpu.make_async_copy(source, place, sem_in.at[n])
        for n, (source, place) in enumerate(((ct, held_ct), (qt, held_qt), (qkv, held_qkv)))
    ]
    for copy in ins:
        copy.start()
    outs = []

    def leave(source, target):
        copy = pltpu.make_async_copy(source, target, sem_out.at[len(outs)])
        copy.start()
        outs.append(copy)

    ins[0].wait()
    for clip in range(2):
        slabs[clip] = fold_text(held_ct[clip])
    for s in range(8):
        leave(slabs.at[s % 2], out.at[s, 3])
    ins[1].wait()
    leave(held_qt.at[zl], own)
    leave(held_qt.at[1 - zl], other)
    ins[2].wait()
    for s, clip, half, cols in head_pieces():
        leave(
            held_qkv.at[clip, :, :, cols],
            out.at[s, pl.ds(0, 3), :, pl.ds(256 * half, 256)],
        )
    for copy in outs:
        copy.wait()


def pack(idx, qkv, qt, ct):
    return pl.pallas_call(
        pack_kernel,
        out_shape=[shape_of(8, 4, BLK, 512)] + [shape_of(3, TXT, 256)] * 2,
        in_specs=[SMEM, ANY, ANY, ANY],
        out_specs=[ANY] * 3,
        scratch_shapes=[pltpu.VMEM(v.shape, BF) for v in (qkv, qt, ct)]
        + [pltpu.VMEM((2, BLK, 512), BF)]
        + [pltpu.SemaphoreType.DMA((3,)), pltpu.SemaphoreType.DMA((26,))],
        compiler_params=params(60),
        cost_estimate=cost(0, 8 * MB),
        name="pack",
    )(idx, qkv, qt, ct)


def unpack_kernel(idx, chunks, own, other, *rest):
    out_video, out_text, video, text, sem = rest
    zl = idx[1]
    copies = []

    def enter(source, target):
        copy = pltpu.make_async_copy(source, target, sem.at[len(copies)])
        copy.start()
        copies.append(copy)

    for s, clip, half, cols in head_pieces():
        enter(chunks.at[s, :, :, pl.ds(256 * half, 256)], video.at[clip, :, :, cols])
    enter(own, text.at[zl])
    enter(other, text.at[1 - zl])
    for copy in copies:
        copy.wait()
    copies = [
        pltpu.make_async_copy(video, out_video, sem.at[0]),
        pltpu.make_async_copy(text, out_text, sem.at[1]),
    ]
    for copy in copies:
        copy.start()
    for copy in copies:
        copy.wait()


def unpack(idx, chunks, own, other):
    outs = [shape_of(2, 3, BLK, 2048), shape_of(2, 3, TXT, 256)]
    return pl.pallas_call(
        unpack_kernel,
        out_shape=outs,
        in_specs=[SMEM, ANY, ANY, ANY],
        out_specs=[ANY] * 2,
        scratch_shapes=[pltpu.VMEM(v.shape, BF) for v in outs]
        + [pltpu.SemaphoreType.DMA((18,))],
        compiler_params=params(60),
        cost_estimate=cost(0, 6 * MB),
        name="unpack",
    )(idx, chunks, own, other)


def normed_rows(raw, gain):
    wide = raw.astype(F32)
    inverse = lax.rsqrt(jnp.mean(wide * wide, axis=-1, keepdims=True) + 1e-6)
    unit = wide * inverse
    return unit, inverse, (unit * gain).astype(BF)


def joint_rows(idx, chunks, text, part):
    return jnp.concatenate([chunks[place_of(idx, k), part] for k in range(8)], axis=0), text[part]


def dot(a, b, dims):
    return lax.dot_general(a, b, (dims, ((), ())), preferred_element_type=F32)


NN = ((1,), (0,))
NT = ((1,), (1,))
TN = ((0,), (0,))


def forward_kernel(idx, length, gains, chunks, own, other, prob_out, att_video, att_text):
    text = jnp.where(pl.program_id(0) < 2, own[...], other[...])
    normed = []
    for part in range(2):
        video_raw, text_raw = joint_rows(idx, chunks, text, part)
        normed.append(
            jnp.concatenate(
                [
                    normed_rows(video_raw, gains[0, part : part + 1])[2],
                    normed_rows(text_raw, gains[1, part : part + 1])[2],
                ],
                axis=0,
            )
        )
    values = jnp.concatenate(joint_rows(idx, chunks, text, 2), axis=0)
    scores = dot(normed[0], normed[1], NT) * SCALE
    seen = lax.broadcasted_iota(jnp.int32, (SEQ, TXT), 1) < length[0]
    scores = jnp.concatenate(
        [scores[:, :VID], jnp.where(seen, scores[:, VID:], -1e30)], axis=1
    )
    powers = jnp.exp(scores - jnp.max(scores, axis=-1, keepdims=True))
    prob = powers * (1.0 / jnp.sum(powers, axis=-1, keepdims=True))
    prob_out[0] = prob
    attended = dot(prob.astype(BF), values, NN).astype(BF)
    att_video[...] = attended[:VID]
    att_text[...] = attended[VID:]


CHUNK = pl.BlockSpec((8, 3, BLK, DH), lambda h: (0, 0, 0, h))
FIRST = pl.BlockSpec((3, TXT, DH), lambda h: (0, 0, jnp.minimum(h, 1)))
LATER = pl.BlockSpec((3, TXT, DH), lambda h: (0, 0, jnp.maximum(h - 2, 0)))
GAINS = pl.BlockSpec((2, 2, DH), lambda h: (0, 0, 0))
PROB = pl.BlockSpec((1, SEQ, SEQ), lambda h: (h, 0, 0))


def forward(idx, length, gains, chunks, own, other):
    return pl.pallas_call(
        forward_kernel,
        grid=(4,),
        out_shape=[shape_of(4, SEQ, SEQ, dtype=F32), shape_of(VID, 512), shape_of(TXT, 512)],
        in_specs=[SMEM, SMEM, GAINS, CHUNK, FIRST, LATER],
        out_specs=[
            PROB,
            pl.BlockSpec((VID, DH), lambda h: (0, h)),
            pl.BlockSpec((TXT, DH), lambda h: (0, h)),
        ],
        compiler_params=params(60),
        cost_estimate=cost(4 * 4 * SEQ * SEQ * DH, 18 * MB, 4 * SEQ * SEQ),
        name="forward",
    )(idx, length, gains, chunks, own, other)


def norm_back(unit, inverse, gain, incoming):
    scaled = incoming * gain
    return inverse * (scaled - unit * jnp.mean(scaled * unit, axis=-1, keepdims=True))


def backward_kernel(
    idx, gains, prob_ref, grad_out, chunks, own, other, outs, out_own, out_other
):
    head = pl.program_id(0)
    text = jnp.where(head < 2, own[...], other[...])
    units = []
    normed = []
    for part in range(2):
        video_raw, text_raw = joint_rows(idx, chunks, text, part)
        v = normed_rows(video_raw, gains[0, part : part + 1])
        t = normed_rows(text_raw, gains[1, part : part + 1])
        units.append((v, t))
        normed.append(jnp.concatenate([v[2], t[2]], axis=0))
    values = jnp.concatenate(joint_rows(idx, chunks, text, 2), axis=0)
    prob = prob_ref[0]
    rows = grad_out[...]
    grad_prob = dot(rows, values, NT)
    inner = jnp.sum(prob * grad_prob, axis=-1, keepdims=True)
    low = (prob * (grad_prob - inner) * SCALE).astype(BF)
    grad_q = dot(low, normed[1], NN)
    grad_k = dot(normed[0], low, TN).T
    grad_v = dot(rows, prob.astype(BF), TN).T
    results = []
    for part, grad in enumerate((grad_q, grad_k)):
        v, t = units[part]
        results.append(
            (
                norm_back(v[0], v[1], gains[0, part : part + 1], grad[:VID]).astype(BF),
                norm_back(t[0], t[1], gains[1, part : part + 1], grad[VID:]).astype(BF),
            )
        )
    results.append((grad_v[:VID].astype(BF), grad_v[VID:].astype(BF)))
    for part in range(3):
        for k in range(8):
            outs[place_of(idx, k), part] = results[part][0][k * BLK : (k + 1) * BLK]

    @pl.when(head < 2)
    def _():
        for part in range(3):
            out_own[part] = results[part][1]

    @pl.when(head >= 2)
    def _():
        for part in range(3):
            out_other[part] = results[part][1]


def backward(idx, gains, prob, grad_out, chunks, own, other):
    return pl.pallas_call(
        backward_kernel,
        grid=(4,),
        out_shape=[shape_of(8, 3, BLK, 512)] + [shape_of(3, TXT, 256)] * 2,
        in_specs=[SMEM, GAINS, PROB, pl.BlockSpec((SEQ, DH), lambda h: (0, h))]
        + [CHUNK, FIRST, LATER],
        out_specs=[CHUNK, FIRST, LATER],
        compiler_params=params(60),
        cost_estimate=cost(4 * 8 * SEQ * SEQ * DH, 20 * MB),
        name="backward",
    )(idx, gains, prob, grad_out, chunks, own, other)


def grad_out_kernel(idx, *refs):
    cots, cot_text, mine, theirs, out, acc = refs[:8], *refs[8:]
    step = pl.program_id(0)
    video = jnp.concatenate([c[...] for c in cots], axis=0)
    text = jnp.concatenate([unfold_text(cot_text[n]) for n in range(2)], axis=1)

    def add(core_0, core_1):
        for half in range(2):
            cols = slice(256 * half, 256 * half + 256)
            for stream, rows, left in ((0, slice(0, VID), video), (1, slice(VID, SEQ), text)):
                weight = jnp.stack(
                    [core_0[:, half, stream], core_1[:, half, stream]], axis=1
                ).reshape(768, 256)
                part = dot(left, weight, NN)
                acc[rows, cols] = jnp.where(step == 0, part, acc[rows, cols] + part)

    @pl.when(idx[2] == 0)
    def _():
        add(mine, theirs)

    @pl.when(idx[2] == 1)
    def _():
        add(theirs, mine)

    @pl.when(step == 3)
    def _():
        out[...] = acc[...].astype(BF)


def project_back(idx, cots, cot_text, mine, theirs):
    weight = pl.BlockSpec((4, 2, 2, BLK, 256), lambda i: (i, 0, 0, 0, 0))
    return pl.pallas_call(
        grad_out_kernel,
        grid=(4,),
        in_specs=[SMEM]
        + [pl.BlockSpec((BLK, 768), lambda i: (0, i))] * 8
        + [pl.BlockSpec((2, None, BLK, 512), lambda i: (i, 3, 0, 0))]
        + [weight, weight],
        out_specs=pl.BlockSpec((SEQ, 512), lambda i: (0, 0)),
        scratch_shapes=[pltpu.VMEM((SEQ, 512), F32)],
        out_shape=shape_of(SEQ, 512),
        compiler_params=params(60),
        cost_estimate=cost(2 * SEQ * 512 * 3072, 13 * MB),
        name="project_back",
    )(idx, *cots, cot_text, mine, theirs)


def weight_grad_kernel(idx, att_video, att_text, cot_text, *refs):
    cots, keep, give = refs[:8], refs[8], refs[9]
    video = jnp.concatenate([c[...] for c in cots], axis=0)
    first = idx[2] == 0
    for stream, (cot, att) in enumerate(
        ((video, att_video), (unfold_text(cot_text[...]), att_text))
    ):
        part = dot(cot, att[...], TN).reshape(2, 2, BLK, 512)
        keep[stream] = jnp.where(first, part[:, 0], part[:, 1]).astype(BF)
        give[stream] = jnp.where(first, part[:, 1], part[:, 0]).astype(BF)


def weight_grad(idx, att_video, att_text, chunks, cots):
    def whole(rows):
        return pl.BlockSpec((rows, 512), lambda i: (0, 0))

    return pl.pallas_call(
        weight_grad_kernel,
        grid=(8,),
        out_shape=[shape_of(2, 16, BLK, 512)] * 2,
        in_specs=[SMEM, whole(VID), whole(TXT)]
        + [pl.BlockSpec((None, None, BLK, 512), lambda i: (i, 3, 0, 0))]
        + [pl.BlockSpec((BLK, 384), lambda i: (0, i))] * 8,
        out_specs=[pl.BlockSpec((2, 2, BLK, 512), lambda i: (0, i, 0, 0))] * 2,
        compiler_params=params(60),
        cost_estimate=cost(2 * SEQ * 512 * 3072, 12 * MB),
        name="weight_grad",
    )(idx, att_video, att_text, chunks, *cots)


def wide_sum(parts):
    return functools.reduce(jnp.add, [p.astype(F32) for p in parts])


def sum_cores(idx, keep, got):
    keep = keep.reshape(2, 4, 4, BLK, 512)
    got = got.reshape(2, 4, 4, BLK, 512)

    def share(step):
        at = lax.rem(idx[4] + step, 4)
        return wide_sum(
            [lax.dynamic_index_in_dim(v, at, axis=2, keepdims=False) for v in (keep, got)]
        )

    return [share(step).astype(BF) for step in range(4)]


def send_x(shares, steps):
    return [send_dp(shares[step], 0, step, 0) for step in steps]


def sum_far_and_near(idx, total, beside):
    def slab(step):
        return lax.dynamic_index_in_dim(
            total, lax.rem(idx[3] + step, 4), axis=1, keepdims=False
        )

    arrived = [send_dp(slab(step), step, 0, 0) for step in (2, 1, 3)]
    total, beside = lax.optimization_barrier((wide_sum([slab(0)] + arrived), beside))
    last = send_sp(total[:, :, 256:].astype(BF), 0, 1)
    total = wide_sum([total[:, :, :256], last])
    return total[0].T, total[1].T, beside


def body(qkv_video, qkv_text, qk_gains, text_len, w_out_video, w_out_text, cot_video, cot_text):
    sp, dp = lax.axis_index("sp"), lax.axis_index("dp")
    y, zl = sp // 2, sp % 2
    idx = jnp.stack([y, zl, dp % 2, dp // 8, (dp // 2) % 4]).astype(jnp.int32)
    length = lax.dynamic_slice(text_len, (zl,), (1,))

    after = lax.optimization_barrier

    def of_clip(array, clip):
        return lax.dynamic_index_in_dim(array, clip, axis=0, keepdims=False)

    cot_own = of_clip(cot_video, zl)
    cot_send = of_clip(cot_video, 1 - zl)
    w_own = jnp.stack([w_out_video.T, w_out_text.T])
    cot_own, cot_send = after((cot_own, cot_send))

    near = [cot_own, send_sp(cot_send, 0, 1)]
    below, above = [send_sp(cot_own, 1, 0)], [send_sp(cot_own, 3, 0)]
    w_pair = jnp.stack([w_own, send_sp(w_own, 0, 1)])
    packed = pack(idx, qkv_video, qkv_text, cot_text)
    near, below, above, packed = after((near, below, above, packed))

    weights = lax.all_gather(
        w_pair,
        "dp",
        axis=0,
        axis_index_groups=[[2 * n + core for n in range(16)] for core in range(2)],
    )
    below = below + [send_sp(near[1], 1, 0)]
    above = above + [send_sp(near[1], 3, 0)]
    sent, text_own, text_send = packed
    text_other = send_sp(text_send, 0, 1)
    chunks = lax.all_to_all(sent, "sp", 0, 0, tiled=True)
    below, above, chunks, text_other = after((below, above, chunks, text_other))

    far = [send_sp(below[0], 1, 0), send_sp(above[1], 3, 0)]
    prob, att_video, att_text = forward(
        idx, length, qk_gains, chunks, text_own, text_other
    )
    att_video, att_text, far = after((att_video, att_text, far))

    cots = near + below + far + above

    keep, give = weight_grad(idx, att_video, att_text, chunks, cots)
    keep, give, weights = after((keep, give, weights))

    other_weights = send_dp(weights, 0, 0, 1)
    give, cots, other_weights = after((give, cots, other_weights))

    got = send_dp(give, 0, 0, 1)
    grad_out = project_back(idx, cots, chunks, weights, other_weights)
    got, keep, grad_out = after((got, keep, grad_out))

    shares = sum_cores(idx, keep, got)
    shares, grad_out = after((shares, grad_out))

    near_sums = send_x(shares, (1, 3))
    grads, own, other = backward(
        idx, qk_gains, prob, grad_out, chunks, text_own, text_other
    )
    near_sums, grads, other, shares = after((near_sums, grads, other, shares))

    far_sums = send_x(shares, (2,))
    grads = lax.all_to_all(grads, "sp", 0, 0, tiled=True)
    other = send_sp(other, 0, 1)
    total = wide_sum([shares[0]] + near_sums + far_sums).astype(BF)
    grad_w_video, grad_w_text, other = sum_far_and_near(idx, total, other)
    grad_qkv_video, grad_qkv_text = unpack(idx, grads, own, other)
    return (grad_qkv_video, grad_qkv_text, grad_w_video, grad_w_text)


def solution(mesh):
    return jax.shard_map(
        body,
        mesh=mesh,
        in_specs=(
            P("dp", None, "sp", None),
            P("dp", None, None, "sp"),
            P(),
            P("dp"),
            P("sp", "dp"),
            P("sp", "dp"),
            P("dp", "sp", None),
            P("dp", None, "sp"),
        ),
        out_specs=(
            P("dp", None, "sp", None),
            P("dp", None, None, "sp"),
            P("sp", "dp"),
            P("sp", "dp"),
        ),
        check_vma=False,
    )
```
